256 devices in a mesh: dp: 32 (over x_hi, z, core), grp: 8 (over y, x_lo).
Axes of the slice: x: 4 (x_hi: 2, x_lo: 2; x = x_hi * 2 + x_lo), y: 4, z: 8, core: 2. Of those that a mesh axis runs over, the one named last changes fastest.
Arguments:
- images: bfloat16 [16384, 1152], P(('dp', 'grp')), may hold values from -24 to 24
- texts: bfloat16 [16384, 1152], P(('dp', 'grp')), may hold values from -24 to 24
- log_scale: float32 [1], replicated, may hold values from 4 to 4.8
- bias: float32 [1], replicated, may hold values from -12 to -8
Outputs:
- image_grad: float32 [16384, 1152], P(('dp', 'grp'))
- text_grad: float32 [16384, 1152], P(('dp', 'grp'))
- stats: float32 [3], replicated
The draws below stay inside these ranges and needn't reach their ends.
All inputs are finite; a program needn't handle non-finite values.
Results may differ from the reference program's by a relative error of at most 0.002.
The reference program's roundings to bfloat16 on the way (of `img_low` and `grad_low`) count: a program that leaves them out, or rounds other values in their place, can miss the bound.
Values may be sent and summed in bfloat16 or wider, within the bound.
No kernel may reach another device: no remote copies, remote signals or barrier semaphores. Data moves between devices by JAX's collectives and lax.ppermute only.
A program may use at most 64 MiB of HBM per device.

```python
import math
import jax
import jax.numpy as jnp
from jax import lax

EMB = 1152
BATCH = 16384


def pair_base(key):
    common = jax.random.truncated_normal(jax.random.fold_in(key, 101), -4.0, 4.0, (BATCH, EMB), jnp.float32)
    base = common
    mix = jax.random.uniform(jax.random.fold_in(key, 102), (BATCH, 1), jnp.float32, 0.0, 0.25)
    return (base, mix)


def row_scales(key, top):
    return jnp.exp(jax.random.uniform(key, (BATCH, 1), jnp.float32, -jnp.log(top), jnp.log(top)))


def draw_images(key, part):
    base, mix = pair_base(key)
    top = 2.0
    key = jax.random.fold_in(key, 3)
    return (base * row_scales(key, top)).astype(jnp.bfloat16)


def draw_texts(key, part):
    base, mix = pair_base(key)
    top = 2.0
    noise = jax.random.truncated_normal(jax.random.fold_in(key, 5), -4.0, 4.0, (BATCH, EMB), jnp.float32)
    key = jax.random.fold_in(key, 7)
    values = mix * base + jnp.sqrt(1.0 - mix * mix) * noise
    return (values * row_scales(key, top)).astype(jnp.bfloat16)


def setup_inputs(seed: int = 0) -> dict:
    key_list = jax.random.split(jax.random.key(seed), 5)
    images = draw_images(jax.random.fold_in(key_list[4], 71), 0)
    texts = draw_texts(jax.random.fold_in(key_list[4], 71), 0)
    log_scale = jnp.clip(jax.random.uniform(key_list[2], (1,), jnp.float32, 4.0, 4.8), 4.0, 4.8)
    bias = jnp.clip(jax.random.uniform(key_list[3], (1,), jnp.float32, -12.0, -8.0), -12.0, -8.0)
    return {"images": images, "texts": texts, "log_scale": log_scale, "bias": bias}


EPS = 1e-06

def normalize(rows):
    values = rows.astype(jnp.float32)
    norms = jnp.sqrt(lax.optimization_barrier(jnp.sum(values * values, axis=-1, keepdims=True)) + EPS)
    return (values / norms, norms)

def project(direction, unit, norms):
    along = lax.optimization_barrier(jnp.sum(direction * unit, axis=-1, keepdims=True))
    return (direction - unit * along) / norms

def reference(images, texts, log_scale, bias):
    img_unit, img_norm = normalize(images)
    txt_unit, txt_norm = normalize(texts)
    img_low = img_unit.astype(jnp.bfloat16)
    txt_low = txt_unit.astype(jnp.bfloat16)
    scale = jnp.exp(log_scale[0])
    shift = bias[0]
    block = math.gcd(512, BATCH)
    blocks = img_low.reshape(BATCH // block, block, EMB)
    starts = (jnp.arange(BATCH // block) * block).astype(jnp.int32)
    txt_pos = lax.broadcasted_iota(jnp.int32, (1, BATCH), 1)

    def step(carry, item):
        txt_acc, sums = carry
        rows, start = item
        cosine = jnp.dot(rows, txt_low.T, preferred_element_type=jnp.float32)
        scaled = scale * cosine
        logits = scaled + shift
        img_pos = start + lax.broadcasted_iota(jnp.int32, (block, 1), 0)
        positive = img_pos == txt_pos
        sign = jnp.where(positive, 1.0, -1.0).astype(jnp.float32)
        losses = jax.nn.softplus(-sign * logits)
        grad = jax.nn.sigmoid(logits) - positive.astype(jnp.float32)
        grad_low = grad.astype(jnp.bfloat16)
        img_part = jnp.dot(grad_low, txt_low, preferred_element_type=jnp.float32)
        txt_acc = txt_acc + jnp.dot(grad_low.T, rows, preferred_element_type=jnp.float32)
        part_sums = jnp.stack([jnp.sum(losses), jnp.sum(grad * scaled), jnp.sum(grad)])
        return ((txt_acc, sums + part_sums), img_part)
    init = (jnp.zeros((BATCH, EMB), jnp.float32), jnp.zeros((3,), jnp.float32))
    (txt_acc, sums), img_parts = lax.scan(step, init, (blocks, starts))
    img_dir = scale * img_parts.reshape(BATCH, EMB)
    txt_dir = scale * txt_acc
    image_grad = project(img_dir, img_unit, img_norm)
    text_grad = project(txt_dir, txt_unit, txt_norm)
    return (image_grad, text_grad, sums / BATCH)
```

```python
import jax
import jax.numpy as jnp
from jax import lax
from jax.experimental import pallas as pl
from jax.experimental.pallas import tpu as pltpu
from jax.sharding import Mesh
from jax.sharding import PartitionSpec as P

EPS = 1e-06
AXES = ("x_hi", "z", "core", "y", "x_lo")
SIZES = (2, 8, 2, 4, 2)
PLANE = ("x_hi", "y", "x_lo")
PEERS = 16
DEPTH = 8
BF16 = jnp.bfloat16
F32 = jnp.float32
VMEM = pl.BlockSpec(memory_space=pltpu.VMEM)
SMEM = pl.BlockSpec(memory_space=pltpu.SMEM)
PARAMS = pltpu.CompilerParams(vmem_limit_bytes=48 * 1024 * 1024)


def cost(flops, nbytes):
    return pl.CostEstimate(flops=flops, bytes_accessed=nbytes, transcendentals=0)


def place(index):
    out = []
    for size in reversed(SIZES):
        out.append(index % size)
        index //= size
    return list(reversed(out))


def number(where):
    index = 0
    for size, at in zip(SIZES, where):
        index = index * size + at
    return index


def shifted(array, axis, by):
    pairs = []
    for source in range(256):
        where = place(source)
        where[axis] = (where[axis] + by) % SIZES[axis]
        pairs.append((source, number(where)))
    return lax.ppermute(array, AXES, pairs)


def flipped(array, axis, by):
    pairs = []
    for source in range(256):
        where = place(source)
        where[axis] ^= by
        pairs.append((source, number(where)))
    return lax.ppermute(array, AXES, pairs)


def along_z(array, by):
    return shifted(array, 1, by)


def other_core(array):
    return shifted(array, 2, 1)


def unit_of(ref):
    values = ref[...].astype(F32)
    norms = jnp.sqrt(jnp.sum(values * values, axis=-1, keepdims=True) + EPS)
    return values / norms, norms


def copies_kernel(rows_ref, out_ref):
    low = unit_of(rows_ref)[0].astype(BF16)
    for k in range(PEERS):
        out_ref[k] = low


def low_kernel(rows_ref, out_ref):
    out_ref[...] = unit_of(rows_ref)[0].astype(BF16)


def fold_sum(array):
    return jnp.sum(array.reshape(-1, 8, array.shape[-1]), axis=0)


def fold_growth(array):
    parts = array.reshape(-1, 8, array.shape[-1])
    while parts.shape[0] > 1:
        half = parts.shape[0] // 2
        a, b = parts[:half], parts[half:]
        parts = a + (b + a * b)
    return parts[0]


def lanes(array):
    out = array[:, :128]
    for at in range(128, array.shape[-1], 128):
        out = out + array[:, at : at + 128]
    return out


def pair_kernel(first_ref, scale_ref, shift_ref, img_ref, mine_ref, theirs_ref, grad_ref, sums_ref):
    tile = pl.program_id(0)
    rows = img_ref.shape[0]
    half = mine_ref.shape[0]
    wide = 256
    scale = scale_ref[0]
    shift = shift_ref[0]
    imgs = img_ref[...]
    loss_sum = jnp.zeros((8, 128), F32)
    scaled_sum = jnp.zeros((8, 128), F32)
    grad_sum = jnp.zeros((8, 128), F32)
    for side, txt_ref in enumerate((mine_ref, theirs_ref)):
        for at in range(0, half, wide):
            cosine = lax.dot_general(
                imgs, txt_ref[at : at + wide, :], (((1,), (1,)), ((), ())), preferred_element_type=F32
            )
            scaled = scale * cosine
            logits = scaled + shift
            small = jnp.exp(-jnp.abs(logits))
            whole = 1.0 + small
            grad = jnp.where(logits >= 0.0, 1.0, small) / whole
            signed = logits
            if side == 0 and at == 0:
                row = lax.broadcasted_iota(jnp.int32, (rows, wide), 0) + (tile * rows - first_ref[0])
                col = lax.broadcasted_iota(jnp.int32, (rows, wide), 1)
                positive = (row == col) & (col < 64)
                signed = jnp.where(positive, -logits, logits)
                grad = jnp.where(positive, grad - 1.0, grad)
            loss_sum += lanes(fold_sum(jnp.maximum(signed, 0.0)) + jnp.log1p(fold_growth(small)))
            scaled_sum += lanes(fold_sum(grad * scaled))
            grad_sum += lanes(fold_sum(grad))
            grad_ref[:, side * half + at : side * half + at + wide] = grad.astype(BF16)

    @pl.when(tile == 0)
    def _():
        sums_ref[...] = jnp.zeros_like(sums_ref)

    sums_ref[0:8, :] += loss_sum
    sums_ref[8:16, :] += scaled_sum
    sums_ref[16:24, :] += grad_sum


def pairs(first, scale, shift, imgs, mine, theirs):
    count, emb = imgs.shape
    half = mine.shape[0]
    rows = 256
    return pl.pallas_call(
        pair_kernel,
        grid=(count // rows,),
        in_specs=[
            SMEM,
            SMEM,
            SMEM,
            pl.BlockSpec((rows, emb), lambda i: (i, 0)),
            pl.BlockSpec((half, emb), lambda i: (0, 0)),
            pl.BlockSpec((half, emb), lambda i: (0, 0)),
        ],
        out_specs=[
            pl.BlockSpec((rows, 2 * half), lambda i: (i, 0)),
            pl.BlockSpec((24, 128), lambda i: (0, 0)),
        ],
        out_shape=[
            jax.ShapeDtypeStruct((count, 2 * half), BF16),
            jax.ShapeDtypeStruct((24, 128), F32),
        ],
        compiler_params=PARAMS,
        cost_estimate=cost(2 * count * 2 * half * emb, 8 * 2**20),
    )(first, scale, shift, imgs, mine, theirs)


def project_kernel(scale_ref, rows_ref, parts_ref, out_ref):
    unit, norms = unit_of(rows_ref)
    total = parts_ref[0].astype(F32)
    for k in range(1, parts_ref.shape[0]):
        total = total + parts_ref[k].astype(F32)
    direction = scale_ref[0] * total
    along = jnp.sum(direction * unit, axis=-1, keepdims=True)
    out_ref[...] = (direction - unit * along) / norms


def projected(scale, rows, parts):
    return pl.pallas_call(
        project_kernel,
        in_specs=[SMEM, VMEM, VMEM],
        out_specs=VMEM,
        out_shape=jax.ShapeDtypeStruct(rows.shape, F32),
        compiler_params=PARAMS,
        cost_estimate=cost(10**6, 4 * 2**20),
    )(scale, rows, parts)


def on_device(images, texts, log_scale, bias):
    rows, emb = images.shape
    scale = jnp.exp(log_scale)
    plane = (lax.axis_index("x_hi") * 4 + lax.axis_index("y")) * 2 + lax.axis_index("x_lo")
    first = (plane * rows).astype(jnp.int32).reshape(1)

    copies = pl.pallas_call(
        copies_kernel,
        in_specs=[VMEM],
        out_specs=VMEM,
        out_shape=jax.ShapeDtypeStruct((PEERS, rows, emb), BF16),
        compiler_params=PARAMS,
        cost_estimate=cost(10**6, 3 * 2**20),
    )(images)
    txt_low = pl.pallas_call(
        low_kernel,
        in_specs=[VMEM],
        out_specs=VMEM,
        out_shape=jax.ShapeDtypeStruct((rows, emb), BF16),
        compiler_params=PARAMS,
        cost_estimate=cost(10**6, 2**19),
    )(texts)

    imgs = lax.all_to_all(copies, PLANE, 0, 0).reshape(PEERS * rows, emb)
    up, down = [txt_low], []
    for _ in range(4):
        up.append(along_z(up[-1], 1))
    down.append(along_z(txt_low, -1))
    for _ in range(2):
        down.append(along_z(down[-1], -1))
    mine = jnp.concatenate(up + down[::-1], axis=0)
    theirs = other_core(mine)

    grad_low, sums = pairs(first, scale, bias, imgs, mine, theirs)
    half = DEPTH * rows
    img_part = jnp.dot(grad_low[:, :half], mine, preferred_element_type=F32) + jnp.dot(
        grad_low[:, half:], theirs, preferred_element_type=F32
    )
    img_part = img_part.astype(BF16).reshape(PEERS, rows, emb)
    txt_part = lax.dot_general(grad_low, imgs, (((0,), (0,)), ((), ())), preferred_element_type=F32)

    img_recv = lax.all_to_all(img_part, PLANE, 0, 0)

    blocks = (txt_part[:half] + other_core(txt_part[half:])).reshape(DEPTH, rows, emb)
    left = blocks[4]
    for k in (3, 2, 1):
        left = along_z(left, -1) + blocks[k]
    left = along_z(left, -1)
    right = blocks[5]
    for k in (6, 7):
        right = along_z(right, 1) + blocks[k]
    right = along_z(right, 1)
    txt_total = (blocks[0] + left + right)[None]

    sums = jnp.sum(sums.reshape(3, -1), axis=-1)
    for axis, by in ((2, 1), (1, 4), (1, 2), (1, 1), (0, 1), (3, 2), (3, 1), (4, 1)):
        sums = sums + flipped(sums, axis, by)
    stats = sums / (rows * 256)

    image_grad = projected(scale, images, img_recv)
    text_grad = projected(scale, texts, txt_total)
    return image_grad, text_grad, stats


def solution(mesh):
    fine = Mesh(mesh.devices.reshape(SIZES), AXES)
    whole = P(AXES, None)
    return jax.shard_map(
        on_device, mesh=fine, in_specs=(whole, whole, P(), P()), out_specs=(whole, whole, P()), check_vma=False
    )
```

```python
import jax
import jax.numpy as jnp
from jax import lax
from jax.experimental import pallas as pl
from jax.experimental.pallas import tpu as pltpu
from jax.sharding import Mesh
from jax.sharding import PartitionSpec as P

EPS = 1e-06
AXES = ("x_hi", "z", "core", "y", "x_lo")
SIZES = (2, 8, 2, 4, 2)
PLANE = ("x_hi", "y", "x_lo")
PEERS = 16
DEPTH = 8
BF16 = jnp.bfloat16
F32 = jnp.float32
F16 = jnp.float16
VMEM = pl.BlockSpec(memory_space=pltpu.VMEM)
SMEM = pl.BlockSpec(memory_space=pltpu.SMEM)
PARAMS = pltpu.CompilerParams(vmem_limit_bytes=48 * 1024 * 1024)


def cost(flops, nbytes):
    return pl.CostEstimate(flops=flops, bytes_accessed=nbytes, transcendentals=0)


def place(index):
    out = []
    for size in reversed(SIZES):
        out.append(index % size)
        index //= size
    return list(reversed(out))


def number(where):
    index = 0
    for size, at in zip(SIZES, where):
        index = index * size + at
    return index


def shifted(array, axis, by):
    pairs = []
    for source in range(256):
        where = place(source)
        where[axis] = (where[axis] + by) % SIZES[axis]
        pairs.append((source, number(where)))
    return lax.ppermute(array, AXES, pairs)


def flipped(array, axis, by):
    pairs = []
    for source in range(256):
        where = place(source)
        where[axis] ^= by
        pairs.append((source, number(where)))
    return lax.ppermute(array, AXES, pairs)


def joined(message, arrived):
    return jnp.concatenate([message[:3] + arrived[:3], message[3:], arrived[3:]])


def along_z(array, by):
    return shifted(array, 1, by)


def other_core(array):
    return shifted(array, 2, 1)


def unit_of(ref):
    values = ref[...].astype(F32)
    norms = jnp.sqrt(jnp.sum(values * values, axis=-1, keepdims=True) + EPS)
    return values / norms, norms


def copies_kernel(rows_ref, out_ref):
    low = unit_of(rows_ref)[0].astype(BF16)
    for k in range(PEERS):
        out_ref[k] = low


def low_kernel(rows_ref, out_ref):
    out_ref[...] = unit_of(rows_ref)[0].astype(BF16)


def fold_sum(array):
    return jnp.sum(array.reshape(-1, 8, array.shape[-1]), axis=0)


def fold_growth(array):
    parts = array.reshape(-1, 8, array.shape[-1])
    while parts.shape[0] > 1:
        half = parts.shape[0] // 2
        a, b = parts[:half], parts[half:]
        parts = a + (b + a * b)
    return parts[0]


def lanes(array):
    out = array[:, :128]
    for at in range(128, array.shape[-1], 128):
        out = out + array[:, at : at + 128]
    return out


def pair_kernel(first_ref, scale_ref, shift_ref, img_ref, mine_ref, theirs_ref, grad_ref, sums_ref, size_ref, acc_ref):
    tile = pl.program_id(0)
    rows = img_ref.shape[0]
    half = mine_ref.shape[0]
    wide = 256
    scale = scale_ref[0]
    shift = shift_ref[0]
    imgs = img_ref[...]
    loss_sum = jnp.zeros((8, 128), F32)
    scaled_sum = jnp.zeros((8, 128), F32)
    grad_sum = jnp.zeros((8, 128), F32)
    size_sum = jnp.zeros((8, 128), F32)
    for side, txt_ref in enumerate((mine_ref, theirs_ref)):
        for at in range(0, half, wide):
            cosine = lax.dot_general(
                imgs, txt_ref[at : at + wide, :], (((1,), (1,)), ((), ())), preferred_element_type=F32
            )
            scaled = scale * cosine
            logits = scaled + shift
            small = jnp.exp(-jnp.abs(logits))
            whole = 1.0 + small
            grad = jnp.where(logits >= 0.0, 1.0, small) / whole
            signed = logits
            if side == 0 and at == 0:
                row = lax.broadcasted_iota(jnp.int32, (rows, wide), 0) + (tile * rows - first_ref[0])
                col = lax.broadcasted_iota(jnp.int32, (rows, wide), 1)
                positive = (row == col) & (col < 64)
                signed = jnp.where(positive, -logits, logits)
                grad = jnp.where(positive, grad - 1.0, grad)
            loss_sum += lanes(fold_sum(jnp.maximum(signed, 0.0)) + jnp.log1p(fold_growth(small)))
            scaled_sum += lanes(fold_sum(grad * scaled))
            part = lanes(fold_sum(grad))
            grad_sum += part
            size_sum += lanes(fold_sum(jnp.abs(grad))) if side == 0 and at == 0 else part
            grad_ref[:, side * half + at : side * half + at + wide] = grad.astype(BF16)

    @pl.when(tile == 0)
    def _():
        acc_ref[...] = jnp.zeros_like(acc_ref)

    acc_ref[0] += loss_sum
    acc_ref[1] += scaled_sum
    acc_ref[2] += grad_sum
    acc_ref[3] += size_sum

    @pl.when(tile == pl.num_programs(0) - 1)
    def _():
        for k in range(3):
            sums_ref[k] = jnp.sum(acc_ref[k])
        size_ref[0] = jnp.sum(acc_ref[3])


def pairs(first, scale, shift, imgs, mine, theirs):
    count, emb = imgs.shape
    half = mine.shape[0]
    rows = 256
    return pl.pallas_call(
        pair_kernel,
        grid=(count // rows,),
        in_specs=[
            SMEM,
            SMEM,
            SMEM,
            pl.BlockSpec((rows, emb), lambda i: (i, 0)),
            pl.BlockSpec((half, emb), lambda i: (0, 0)),
            pl.BlockSpec((half, emb), lambda i: (0, 0)),
        ],
        out_specs=[
            pl.BlockSpec((rows, 2 * half), lambda i: (i, 0)),
            SMEM,
            SMEM,
        ],
        out_shape=[
            jax.ShapeDtypeStruct((count, 2 * half), BF16),
            jax.ShapeDtypeStruct((3,), F32),
            jax.ShapeDtypeStruct((1,), F32),
        ],
        scratch_shapes=[pltpu.VMEM((4, 8, 128), F32)],
        compiler_params=PARAMS,
        cost_estimate=cost(2 * count * 2 * half * emb, 8 * 2**20),
    )(first, scale, shift, imgs, mine, theirs)


def project_kernel(scale_ref, rows_ref, total_ref, out_ref):
    unit, norms = unit_of(rows_ref)
    direction = scale_ref[0] * total_ref[...]
    along = jnp.sum(direction * unit, axis=-1, keepdims=True)
    out_ref[...] = (direction - unit * along) / norms


def projected(scale, rows, total):
    return pl.pallas_call(
        project_kernel,
        in_specs=[SMEM, VMEM, VMEM],
        out_specs=VMEM,
        out_shape=jax.ShapeDtypeStruct(rows.shape, F32),
        compiler_params=PARAMS,
        cost_estimate=cost(10**6, 4 * 2**20),
    )(scale, rows, total)


def on_device(images, texts, log_scale, bias):
    rows, emb = images.shape
    scale = jnp.exp(log_scale)
    plane = (lax.axis_index("x_hi") * 4 + lax.axis_index("y")) * 2 + lax.axis_index("x_lo")
    first = (plane * rows).astype(jnp.int32).reshape(1)

    copies = pl.pallas_call(
        copies_kernel,
        in_specs=[VMEM],
        out_specs=VMEM,
        out_shape=jax.ShapeDtypeStruct((PEERS, rows, emb), BF16),
        compiler_params=PARAMS,
        cost_estimate=cost(10**6, 3 * 2**20),
    )(images)
    copies, texts_later = lax.optimization_barrier((copies, texts))
    txt_low = pl.pallas_call(
        low_kernel,
        in_specs=[VMEM],
        out_specs=VMEM,
        out_shape=jax.ShapeDtypeStruct((rows, emb), BF16),
        compiler_params=PARAMS,
        cost_estimate=cost(10**6, 2**19),
    )(texts_later)

    imgs = lax.all_to_all(copies, PLANE, 0, 0).reshape(PEERS * rows, emb)
    up, down = [txt_low], []
    for _ in range(4):
        up.append(along_z(up[-1], 1))
    down.append(along_z(txt_low, -1))
    for _ in range(2):
        down.append(along_z(down[-1], -1))
    mine = jnp.concatenate(up + down[::-1], axis=0)
    theirs = other_core(mine)

    grad_low, sums, size = pairs(first, scale, bias, imgs, mine, theirs)
    message = jnp.concatenate([sums, size])

    half = DEPTH * rows
    arrived = flipped(message, 3, 2)
    factor = 16384.0 / jnp.maximum(size[0], 1e-30)
    img_part = jnp.dot(grad_low[:, :half], mine, preferred_element_type=F32) + jnp.dot(
        grad_low[:, half:], theirs, preferred_element_type=F32
    )
    img_part = (img_part * factor).astype(F16).reshape(PEERS, rows, emb)
    img_part, grad_low, arrived = lax.optimization_barrier((img_part, grad_low, arrived))
    img_recv = lax.all_to_all(img_part, PLANE, 0, 0)
    message = joined(message, arrived)

    arrived = flipped(message, 3, 1)
    txt_part = lax.dot_general(grad_low, imgs, (((0,), (0,)), ((), ())), preferred_element_type=F32)
    txt_part, arrived = lax.optimization_barrier((txt_part, arrived))
    message = joined(message, arrived)

    blocks = other_core(txt_part[half:])
    arrived = flipped(message, 0, 1)
    blocks, arrived = lax.optimization_barrier((blocks, arrived))
    blocks = (txt_part[:half] + blocks).reshape(DEPTH, rows, emb)
    message = joined(message, arrived)

    left, right = along_z(blocks[4], -1), along_z(blocks[5], 1)
    arrived = flipped(message, 4, 1)
    left, right, arrived = lax.optimization_barrier((left, right, arrived))
    left, right = left + blocks[3], right + blocks[6]
    message = joined(message, arrived)
    sums, sizes = message[:3], message[3:]

    left, right = along_z(left, -1), along_z(right, 1)
    arrived = flipped(sums, 1, 4)
    left, right, arrived = lax.optimization_barrier((left, right, arrived))
    left, right, sums = left + blocks[2], right + blocks[7], sums + arrived

    left, right = along_z(left, -1), along_z(right, 1)
    arrived = flipped(sums, 1, 2)
    left, right, arrived = lax.optimization_barrier((left, right, arrived))
    left, sums = left + blocks[1], sums + arrived

    left = along_z(left, -1)
    arrived = flipped(sums, 1, 1)
    left, arrived = lax.optimization_barrier((left, arrived))
    txt_total, sums = blocks[0] + left + right, sums + arrived
    stats = (sums + flipped(sums, 2, 1)) / (rows * 256)

    mine_at = (lax.axis_index("x_lo") << 3) | (lax.axis_index("x_hi") << 2) | ((lax.axis_index("y") & 1) << 1) | (lax.axis_index("y") >> 1)
    peer = jnp.arange(PEERS)
    peer_at = ((peer & 1) << 3) | ((peer >> 3) << 2) | (((peer >> 1) & 1) << 1) | ((peer >> 2) & 1)
    chosen = (peer_at ^ mine_at)[:, None] == jnp.arange(PEERS)[None, :]
    weights = jnp.sum(jnp.where(chosen, jnp.maximum(sizes, 1e-30)[None, :], 0.0), axis=1) / 16384.0
    img_total = jnp.sum(img_recv.astype(F32) * weights[:, None, None], axis=0)

    image_grad = projected(scale, images, img_total)
    text_grad = projected(scale, texts, txt_total)
    return image_grad, text_grad, stats


def solution(mesh):
    fine = Mesh(mesh.devices.reshape(SIZES), AXES)
    whole = P(AXES, None)
    return jax.shard_map(
        on_device, mesh=fine, in_specs=(whole, whole, P(), P()), out_specs=(whole, whole, P()), check_vma=False
    )
```

```python
import jax
import jax.numpy as jnp
from jax import lax
from jax.experimental import pallas as pl
from jax.experimental.pallas import tpu as pltpu
from jax.sharding import Mesh
from jax.sharding import PartitionSpec as P

EPS = 1e-06
AXES = ("x_hi", "z", "core", "y", "x_lo")
SIZES = (2, 8, 2, 4, 2)
PLANE = ("x_hi", "y", "x_lo")
PEERS = 16
DEPTH = 8
BF16 = jnp.bfloat16
F32 = jnp.float32
F16 = jnp.float16
VMEM = pl.BlockSpec(memory_space=pltpu.VMEM)
SMEM = pl.BlockSpec(memory_space=pltpu.SMEM)
PARAMS = pltpu.CompilerParams(vmem_limit_bytes=48 * 1024 * 1024)


def cost(flops, nbytes):
    return pl.CostEstimate(flops=flops, bytes_accessed=nbytes, transcendentals=0)


def place(index):
    out = []
    for size in reversed(SIZES):
        out.append(index % size)
        index //= size
    return list(reversed(out))


def number(where):
    index = 0
    for size, at in zip(SIZES, where):
        index = index * size + at
    return index


def shifted(array, axis, by):
    pairs = []
    for source in range(256):
        where = place(source)
        where[axis] = (where[axis] + by) % SIZES[axis]
        pairs.append((source, number(where)))
    return lax.ppermute(array, AXES, pairs)


def flipped(array, axis, by):
    pairs = []
    for source in range(256):
        where = place(source)
        where[axis] ^= by
        pairs.append((source, number(where)))
    return lax.ppermute(array, AXES, pairs)


def moved(array, dx, dy):
    pairs = []
    for source in range(256):
        x_hi, z, core, y, x_lo = place(source)
        x = (x_hi * 2 + x_lo + dx) % 4
        pairs.append((source, number((x // 2, z, core, (y + dy) % 4, x % 2))))
    return lax.ppermute(array, AXES, pairs)


def joined(message, arrived):
    sums = message[:3]
    for other in arrived:
        sums = sums + other[:3]
    return jnp.concatenate([sums, message[3:]] + [other[3:] for other in arrived])


def along_z(array, by):
    return shifted(array, 1, by)


def other_core(array):
    return shifted(array, 2, 1)


def unit_of(ref):
    values = ref[...].astype(F32)
    norms = jnp.sqrt(jnp.sum(values * values, axis=-1, keepdims=True) + EPS)
    return values / norms, norms


def copies_kernel(rows_ref, out_ref):
    low = unit_of(rows_ref)[0].astype(BF16)
    for k in range(PEERS):
        out_ref[k] = low


def low_kernel(rows_ref, out_ref):
    out_ref[...] = unit_of(rows_ref)[0].astype(BF16)


def fold_sum(array):
    return jnp.sum(array.reshape(-1, 8, array.shape[-1]), axis=0)


def fold_growth(array):
    parts = array.reshape(-1, 8, array.shape[-1])
    while parts.shape[0] > 1:
        half = parts.shape[0] // 2
        a, b = parts[:half], parts[half:]
        parts = a + (b + a * b)
    return parts[0]


def lanes(array):
    out = array[:, :128]
    for at in range(128, array.shape[-1], 128):
        out = out + array[:, at : at + 128]
    return out


def pair_kernel(first_ref, scale_ref, shift_ref, img_ref, mine_ref, theirs_ref, grad_ref, sums_ref, size_ref, acc_ref):
    tile = pl.program_id(0)
    rows = img_ref.shape[0]
    half = mine_ref.shape[0]
    wide = 256
    scale = scale_ref[0]
    shift = shift_ref[0]
    imgs = img_ref[...]
    loss_sum = jnp.zeros((8, 128), F32)
    scaled_sum = jnp.zeros((8, 128), F32)
    grad_sum = jnp.zeros((8, 128), F32)
    size_sum = jnp.zeros((8, 128), F32)
    for side, txt_ref in enumerate((mine_ref, theirs_ref)):
        for at in range(0, half, wide):
            cosine = lax.dot_general(
                imgs, txt_ref[at : at + wide, :], (((1,), (1,)), ((), ())), preferred_element_type=F32
            )
            scaled = scale * cosine
            logits = scaled + shift
            small = jnp.exp(-jnp.abs(logits))
            whole = 1.0 + small
            grad = jnp.where(logits >= 0.0, 1.0, small) / whole
            signed = logits
            if side == 0 and at == 0:
                row = lax.broadcasted_iota(jnp.int32, (rows, wide), 0) + (tile * rows - first_ref[0])
                col = lax.broadcasted_iota(jnp.int32, (rows, wide), 1)
                positive = (row == col) & (col < 64)
                signed = jnp.where(positive, -logits, logits)
                grad = jnp.where(positive, grad - 1.0, grad)
            loss_sum += lanes(fold_sum(jnp.maximum(signed, 0.0)) + jnp.log1p(fold_growth(small)))
            scaled_sum += lanes(fold_sum(grad * scaled))
            part = lanes(fold_sum(grad))
            grad_sum += part
            size_sum += lanes(fold_sum(jnp.abs(grad))) if side == 0 and at == 0 else part
            grad_ref[:, side * half + at : side * half + at + wide] = grad.astype(BF16)

    @pl.when(tile == 0)
    def _():
        acc_ref[...] = jnp.zeros_like(acc_ref)

    acc_ref[0] += loss_sum
    acc_ref[1] += scaled_sum
    acc_ref[2] += grad_sum
    acc_ref[3] += size_sum

    @pl.when(tile == pl.num_programs(0) - 1)
    def _():
        for k in range(3):
            sums_ref[k] = jnp.sum(acc_ref[k])
        size_ref[0] = jnp.sum(acc_ref[3])


def pairs(first, scale, shift, imgs, mine, theirs):
    count, emb = imgs.shape
    half = mine.shape[0]
    rows = 256
    return pl.pallas_call(
        pair_kernel,
        grid=(count // rows,),
        in_specs=[
            SMEM,
            SMEM,
            SMEM,
            pl.BlockSpec((rows, emb), lambda i: (i, 0)),
            pl.BlockSpec((half, emb), lambda i: (0, 0)),
            pl.BlockSpec((half, emb), lambda i: (0, 0)),
        ],
        out_specs=[
            pl.BlockSpec((rows, 2 * half), lambda i: (i, 0)),
            SMEM,
            SMEM,
        ],
        out_shape=[
            jax.ShapeDtypeStruct((count, 2 * half), BF16),
            jax.ShapeDtypeStruct((3,), F32),
            jax.ShapeDtypeStruct((1,), F32),
        ],
        scratch_shapes=[pltpu.VMEM((4, 8, 128), F32)],
        compiler_params=PARAMS,
        cost_estimate=cost(2 * count * 2 * half * emb, 8 * 2**20),
    )(first, scale, shift, imgs, mine, theirs)


def project_kernel(scale_ref, rows_ref, total_ref, out_ref):
    unit, norms = unit_of(rows_ref)
    direction = scale_ref[0] * total_ref[...]
    along = jnp.sum(direction * unit, axis=-1, keepdims=True)
    out_ref[...] = (direction - unit * along) / norms


def projected(scale, rows, total):
    return pl.pallas_call(
        project_kernel,
        in_specs=[SMEM, VMEM, VMEM],
        out_specs=VMEM,
        out_shape=jax.ShapeDtypeStruct(rows.shape, F32),
        compiler_params=PARAMS,
        cost_estimate=cost(10**6, 4 * 2**20),
    )(scale, rows, total)


def on_device(images, texts, log_scale, bias):
    rows, emb = images.shape
    scale = jnp.exp(log_scale)
    plane = (lax.axis_index("x_hi") * 4 + lax.axis_index("y")) * 2 + lax.axis_index("x_lo")
    first = (plane * rows).astype(jnp.int32).reshape(1)

    copies = pl.pallas_call(
        copies_kernel,
        in_specs=[VMEM],
        out_specs=VMEM,
        out_shape=jax.ShapeDtypeStruct((PEERS, rows, emb), BF16),
        compiler_params=PARAMS,
        cost_estimate=cost(10**6, 3 * 2**20),
    )(images)
    copies, texts_later = lax.optimization_barrier((copies, texts))
    txt_low = pl.pallas_call(
        low_kernel,
        in_specs=[VMEM],
        out_specs=VMEM,
        out_shape=jax.ShapeDtypeStruct((rows, emb), BF16),
        compiler_params=PARAMS,
        cost_estimate=cost(10**6, 2**19),
    )(texts_later)

    imgs = lax.all_to_all(copies, PLANE, 0, 0).reshape(PEERS * rows, emb)
    up, down = [txt_low], []
    for _ in range(4):
        up.append(along_z(up[-1], 1))
    down.append(along_z(txt_low, -1))
    for _ in range(2):
        down.append(along_z(down[-1], -1))
    mine = jnp.concatenate(up + down[::-1], axis=0)
    theirs = other_core(mine)

    grad_low, sums, size = pairs(first, scale, bias, imgs, mine, theirs)
    half = DEPTH * rows

    message = jnp.concatenate([sums, size])
    arrived = [moved(message, by, 0) for by in (1, 2, 3)]
    txt_part = lax.dot_general(grad_low, imgs, (((0,), (0,)), ((), ())), preferred_element_type=F32)
    txt_part, grad_low, *arrived = lax.optimization_barrier((txt_part, grad_low, *arrived))
    message = joined(message, arrived)

    arrived = [moved(message, 0, by) for by in (1, 2, 3)]
    factor = 16384.0 / jnp.maximum(size[0], 1e-30)
    img_part = jnp.dot(grad_low[:, :half], mine, preferred_element_type=F32) + jnp.dot(
        grad_low[:, half:], theirs, preferred_element_type=F32
    )
    img_part = (img_part * factor).astype(F16).reshape(PEERS, rows, emb)
    img_part, *arrived = lax.optimization_barrier((img_part, *arrived))
    img_recv = lax.all_to_all(img_part, PLANE, 0, 0)
    message = joined(message, arrived)
    sums, sizes = message[:3], message[3:]

    blocks = (txt_part[:half] + other_core(txt_part[half:])).reshape(DEPTH, rows, emb)
    left, right = along_z(blocks[4], -1), along_z(blocks[5], 1)
    arrived = flipped(sums, 1, 4)
    left, right, arrived = lax.optimization_barrier((left, right, arrived))
    left, right, sums = left + blocks[3], right + blocks[6], sums + arrived

    left, right = along_z(left, -1), along_z(right, 1)
    arrived = flipped(sums, 1, 2)
    left, right, arrived = lax.optimization_barrier((left, right, arrived))
    left, right, sums = left + blocks[2], right + blocks[7], sums + arrived

    left, right = along_z(left, -1), along_z(right, 1)
    arrived = flipped(sums, 1, 1)
    left, right, arrived = lax.optimization_barrier((left, right, arrived))
    left, sums = left + blocks[1], sums + arrived

    left = along_z(left, -1)
    txt_total = blocks[0] + left + right
    stats = (sums + flipped(sums, 2, 1)) / (rows * 256)

    x, y = lax.axis_index("x_hi") * 2 + lax.axis_index("x_lo"), lax.axis_index("y")
    peer = jnp.arange(PEERS)
    peer_x, peer_y = (peer >> 3) * 2 + (peer & 1), (peer >> 1) & 3
    entry = ((y - peer_y) & 3) * 4 + ((x - peer_x) & 3)
    chosen = entry[:, None] == peer[None, :]
    weights = jnp.sum(jnp.where(chosen, jnp.maximum(sizes, 1e-30)[None, :], 0.0), axis=1) / 16384.0
    img_total = jnp.sum(img_recv.astype(F32) * weights[:, None, None], axis=0)

    image_grad = projected(scale, images, img_total)
    text_grad = projected(scale, texts, txt_total)
    return image_grad, text_grad, stats


def solution(mesh):
    fine = Mesh(mesh.devices.reshape(SIZES), AXES)
    whole = P(AXES, None)
    return jax.shard_map(
        on_device, mesh=fine, in_specs=(whole, whole, P(), P()), out_specs=(whole, whole, P()), check_vma=False
    )
```

```python
import jax
import jax.numpy as jnp
from jax import lax
from jax.experimental import pallas as pl
from jax.experimental.pallas import tpu as pltpu
from jax.sharding import Mesh
from jax.sharding import PartitionSpec as P

EPS = 1e-06
AXES = ("x_hi", "z", "core", "y", "x_lo")
SIZES = (2, 8, 2, 4, 2)
PLANE = ("x_hi", "y", "x_lo")
PEERS = 16
DEPTH = 8
CODE = 1024.0
BF16 = jnp.bfloat16
F32 = jnp.float32
F16 = jnp.float16
VMEM = pl.BlockSpec(memory_space=pltpu.VMEM)
SMEM = pl.BlockSpec(memory_space=pltpu.SMEM)
PARAMS = pltpu.CompilerParams(vmem_limit_bytes=48 * 1024 * 1024)


def cost(flops, nbytes):
    return pl.CostEstimate(flops=flops, bytes_accessed=nbytes, transcendentals=0)


def place(index):
    out = []
    for size in reversed(SIZES):
        out.append(index % size)
        index //= size
    return list(reversed(out))


def number(where):
    index = 0
    for size, at in zip(SIZES, where):
        index = index * size + at
    return index


def shifted(array, axis, by):
    pairs = []
    for source in range(256):
        where = place(source)
        where[axis] = (where[axis] + by) % SIZES[axis]
        pairs.append((source, number(where)))
    return lax.ppermute(array, AXES, pairs)


def flipped(array, axis, by):
    pairs = []
    for source in range(256):
        where = place(source)
        where[axis] ^= by
        pairs.append((source, number(where)))
    return lax.ppermute(array, AXES, pairs)


def moved(array, dx, dy):
    pairs = []
    for source in range(256):
        x_hi, z, core, y, x_lo = place(source)
        x = (x_hi * 2 + x_lo + dx) % 4
        pairs.append((source, number((x // 2, z, core, (y + dy) % 4, x % 2))))
    return lax.ppermute(array, AXES, pairs)


def coded(array):
    return (array * lax.rsqrt(jnp.maximum(jnp.abs(array), 1e-36)) * CODE).astype(F16)


def decoded(array):
    wide = array.astype(F32) * (1.0 / CODE)
    return wide * jnp.abs(wide)


def along_z(array, by):
    return shifted(array, 1, by)


def other_core(array):
    return shifted(array, 2, 1)


def unit_of(ref):
    values = ref[...].astype(F32)
    norms = jnp.sqrt(jnp.sum(values * values, axis=-1, keepdims=True) + EPS)
    return values / norms, norms


def copies_kernel(rows_ref, out_ref):
    low = unit_of(rows_ref)[0].astype(BF16)
    for k in range(PEERS):
        out_ref[k] = low


def low_kernel(rows_ref, out_ref):
    out_ref[...] = unit_of(rows_ref)[0].astype(BF16)


def fold_sum(array):
    return jnp.sum(array.reshape(-1, 8, array.shape[-1]), axis=0)


def fold_growth(array):
    parts = array.reshape(-1, 8, array.shape[-1])
    while parts.shape[0] > 1:
        half = parts.shape[0] // 2
        a, b = parts[:half], parts[half:]
        parts = a + (b + a * b)
    return parts[0]


def lanes(array):
    out = array[:, :128]
    for at in range(128, array.shape[-1], 128):
        out = out + array[:, at : at + 128]
    return out


def pair_kernel(first_ref, scale_ref, shift_ref, img_ref, mine_ref, theirs_ref, grad_ref, sums_ref, acc_ref):
    tile = pl.program_id(0)
    rows = img_ref.shape[0]
    half = mine_ref.shape[0]
    wide = 256
    scale = scale_ref[0]
    shift = shift_ref[0]
    imgs = img_ref[...]
    loss_sum = jnp.zeros((8, 128), F32)
    scaled_sum = jnp.zeros((8, 128), F32)
    grad_sum = jnp.zeros((8, 128), F32)
    for side, txt_ref in enumerate((mine_ref, theirs_ref)):
        for at in range(0, half, wide):
            cosine = lax.dot_general(
                imgs, txt_ref[at : at + wide, :], (((1,), (1,)), ((), ())), preferred_element_type=F32
            )
            scaled = scale * cosine
            logits = scaled + shift
            small = jnp.exp(-jnp.abs(logits))
            whole = 1.0 + small
            grad = jnp.where(logits >= 0.0, 1.0, small) / whole
            signed = logits
            if side == 0 and at == 0:
                row = lax.broadcasted_iota(jnp.int32, (rows, wide), 0) + (tile * rows - first_ref[0])
                col = lax.broadcasted_iota(jnp.int32, (rows, wide), 1)
                positive = (row == col) & (col < 64)
                signed = jnp.where(positive, -logits, logits)
                grad = jnp.where(positive, grad - 1.0, grad)
            loss_sum += lanes(fold_sum(jnp.maximum(signed, 0.0)) + jnp.log1p(fold_growth(small)))
            scaled_sum += lanes(fold_sum(grad * scaled))
            grad_sum += lanes(fold_sum(grad))
            grad_ref[:, side * half + at : side * half + at + wide] = grad.astype(BF16)

    @pl.when(tile == 0)
    def _():
        acc_ref[...] = jnp.zeros_like(acc_ref)

    acc_ref[0] += loss_sum
    acc_ref[1] += scaled_sum
    acc_ref[2] += grad_sum

    @pl.when(tile == pl.num_programs(0) - 1)
    def _():
        for k in range(3):
            sums_ref[k] = jnp.sum(acc_ref[k])


def pairs(first, scale, shift, imgs, mine, theirs):
    count, emb = imgs.shape
    half = mine.shape[0]
    rows = 256
    return pl.pallas_call(
        pair_kernel,
        grid=(count // rows,),
        in_specs=[
            SMEM,
            SMEM,
            SMEM,
            pl.BlockSpec((rows, emb), lambda i: (i, 0)),
            pl.BlockSpec((half, emb), lambda i: (0, 0)),
            pl.BlockSpec((half, emb), lambda i: (0, 0)),
        ],
        out_specs=[
            pl.BlockSpec((rows, 2 * half), lambda i: (i, 0)),
            SMEM,
        ],
        out_shape=[
            jax.ShapeDtypeStruct((count, 2 * half), BF16),
            jax.ShapeDtypeStruct((3,), F32),
        ],
        scratch_shapes=[pltpu.VMEM((3, 8, 128), F32)],
        compiler_params=PARAMS,
        cost_estimate=cost(2 * count * 2 * half * emb, 8 * 2**20),
    )(first, scale, shift, imgs, mine, theirs)


def project_kernel(scale_ref, rows_ref, total_ref, out_ref):
    unit, norms = unit_of(rows_ref)
    direction = scale_ref[0] * total_ref[...]
    along = jnp.sum(direction * unit, axis=-1, keepdims=True)
    out_ref[...] = (direction - unit * along) / norms


def projected(scale, rows, total):
    return pl.pallas_call(
        project_kernel,
        in_specs=[SMEM, VMEM, VMEM],
        out_specs=VMEM,
        out_shape=jax.ShapeDtypeStruct(rows.shape, F32),
        compiler_params=PARAMS,
        cost_estimate=cost(10**6, 4 * 2**20),
    )(scale, rows, total)


def on_device(images, texts, log_scale, bias):
    rows, emb = images.shape
    scale = jnp.exp(log_scale)
    plane = (lax.axis_index("x_hi") * 4 + lax.axis_index("y")) * 2 + lax.axis_index("x_lo")
    first = (plane * rows).astype(jnp.int32).reshape(1)

    copies = pl.pallas_call(
        copies_kernel,
        in_specs=[VMEM],
        out_specs=VMEM,
        out_shape=jax.ShapeDtypeStruct((PEERS, rows, emb), BF16),
        compiler_params=PARAMS,
        cost_estimate=cost(10**6, 3 * 2**20),
    )(images)
    copies, texts_later = lax.optimization_barrier((copies, texts))
    txt_low = pl.pallas_call(
        low_kernel,
        in_specs=[VMEM],
        out_specs=VMEM,
        out_shape=jax.ShapeDtypeStruct((rows, emb), BF16),
        compiler_params=PARAMS,
        cost_estimate=cost(10**6, 2**19),
    )(texts_later)

    imgs = lax.all_to_all(copies, PLANE, 0, 0).reshape(PEERS * rows, emb)
    up, down = [txt_low], []
    for _ in range(4):
        up.append(along_z(up[-1], 1))
    down.append(along_z(txt_low, -1))
    for _ in range(2):
        down.append(along_z(down[-1], -1))
    mine = jnp.concatenate(up + down[::-1], axis=0)
    theirs = other_core(mine)

    grad_low, sums = pairs(first, scale, bias, imgs, mine, theirs)
    half = DEPTH * rows

    txt_part = lax.dot_general(grad_low[:, half:], imgs, (((0,), (0,)), ((), ())), preferred_element_type=F32)
    theirs_part = other_core(coded(txt_part))
    mine_part = lax.dot_general(grad_low[:, :half], imgs, (((0,), (0,)), ((), ())), preferred_element_type=F32)

    arrived = [moved(sums, by, 0) for by in (1, 2, 3)]
    img_part = jnp.dot(grad_low[:, :half], mine, preferred_element_type=F32) + jnp.dot(
        grad_low[:, half:], theirs, preferred_element_type=F32
    )
    img_part = coded(img_part).reshape(PEERS, rows, emb)
    img_part, *arrived = lax.optimization_barrier((img_part, *arrived))
    img_recv = lax.all_to_all(img_part, PLANE, 0, 0)
    sums = sums + arrived[0] + arrived[1] + arrived[2]

    mine_part = mine_part.reshape(DEPTH, rows, emb)
    theirs_part = theirs_part.reshape(DEPTH, rows, emb)
    block = lambda k: mine_part[k] + decoded(theirs_part[k])
    left, right = along_z(coded(block(4)), -1), along_z(coded(block(5)), 1)
    arrived = flipped(sums, 1, 4)
    left, right, arrived = lax.optimization_barrier((left, right, arrived))
    left, right, sums = decoded(left) + block(3), decoded(right) + block(6), sums + arrived

    left, right = along_z(coded(left), -1), along_z(coded(right), 1)
    arrived = flipped(sums, 1, 2)
    left, right, arrived = lax.optimization_barrier((left, right, arrived))
    left, right, sums = decoded(left) + block(2), decoded(right) + block(7), sums + arrived

    left, right = along_z(coded(left), -1), along_z(coded(right), 1)
    arrived = flipped(sums, 1, 1)
    left, right, arrived = lax.optimization_barrier((left, right, arrived))
    left, sums = decoded(left) + block(1), sums + arrived

    left = along_z(coded(left), -1)
    arrived = flipped(sums, 2, 1)
    left, arrived = lax.optimization_barrier((left, arrived))
    txt_total = block(0) + decoded(left) + decoded(right)
    sums = sums + arrived

    img_recv, sums = lax.optimization_barrier((img_recv, sums))
    for by in (1, 2, 3):
        arrived = moved(sums, 0, by)
        stats = arrived + (sums if by == 1 else stats)
    stats = stats / (rows * 256)
    img_total = jnp.sum(decoded(img_recv), axis=0)

    image_grad = projected(scale, images, img_total)
    text_grad = projected(scale, texts, txt_total)
    return image_grad, text_grad, stats


def solution(mesh):
    fine = Mesh(mesh.devices.reshape(SIZES), AXES)
    whole = P(AXES, None)
    return jax.shard_map(
        on_device, mesh=fine, in_specs=(whole, whole, P(), P()), out_specs=(whole, whole, P()), check_vma=False
    )
```

```python
import jax
import jax.numpy as jnp
from jax import lax
from jax.experimental import pallas as pl
from jax.experimental.pallas import tpu as pltpu
from jax.sharding import Mesh
from jax.sharding import PartitionSpec as P

EPS = 1e-06
AXES = ("x_hi", "z", "core", "y", "x_lo")
SIZES = (2, 8, 2, 4, 2)
PLANE = ("x_hi", "y", "x_lo")
PEERS = 16
DEPTH = 8
CODE = 1024.0
EXTRA = 8
PAIRS = 1024.0 * 1024.0
BF16 = jnp.bfloat16
F32 = jnp.float32
F16 = jnp.float16
VMEM = pl.BlockSpec(memory_space=pltpu.VMEM)
SMEM = pl.BlockSpec(memory_space=pltpu.SMEM)
PARAMS = pltpu.CompilerParams(vmem_limit_bytes=48 * 1024 * 1024)


def cost(flops, nbytes):
    return pl.CostEstimate(flops=flops, bytes_accessed=nbytes, transcendentals=0)


def place(index):
    out = []
    for size in reversed(SIZES):
        out.append(index % size)
        index //= size
    return list(reversed(out))


def number(where):
    index = 0
    for size, at in zip(SIZES, where):
        index = index * size + at
    return index


def shifted(array, axis, by):
    pairs = []
    for source in range(256):
        where = place(source)
        where[axis] = (where[axis] + by) % SIZES[axis]
        pairs.append((source, number(where)))
    return lax.ppermute(array, AXES, pairs)


def flipped(array, axis, by):
    pairs = []
    for source in range(256):
        where = place(source)
        where[axis] ^= by
        pairs.append((source, number(where)))
    return lax.ppermute(array, AXES, pairs)


def moved(array, dx, dy):
    pairs = []
    for source in range(256):
        x_hi, z, core, y, x_lo = place(source)
        x = (x_hi * 2 + x_lo + dx) % 4
        pairs.append((source, number((x // 2, z, core, (y + dy) % 4, x % 2))))
    return lax.ppermute(array, AXES, pairs)


def coded(array):
    return (array * lax.rsqrt(jnp.maximum(jnp.abs(array), 1e-36)) * CODE).astype(F16)


def decoded(array):
    wide = array.astype(F32) * (1.0 / CODE)
    return wide * jnp.abs(wide)


def along_z(array, by):
    return shifted(array, 1, by)


def other_core(array):
    return shifted(array, 2, 1)


def unit_of(ref):
    values = ref[...].astype(F32)
    norms = jnp.sqrt(jnp.sum(values * values, axis=-1, keepdims=True) + EPS)
    return values / norms, norms


def copies_kernel(rows_ref, out_ref):
    low = unit_of(rows_ref)[0].astype(BF16)
    for k in range(PEERS):
        out_ref[k] = low


def low_kernel(rows_ref, out_ref):
    out_ref[...] = unit_of(rows_ref)[0].astype(BF16)


def fold_sum(array):
    return jnp.sum(array.reshape(-1, 8, array.shape[-1]), axis=0)


def fold_growth(array):
    parts = array.reshape(-1, 8, array.shape[-1])
    while parts.shape[0] > 1:
        half = parts.shape[0] // 2
        a, b = parts[:half], parts[half:]
        parts = a + (b + a * b)
    return parts[0]


def lanes(array):
    out = array[:, :128]
    for at in range(128, array.shape[-1], 128):
        out = out + array[:, at : at + 128]
    return out


def pair_kernel(first_ref, scale_ref, shift_ref, img_ref, mine_ref, theirs_ref, grad_ref, sums_ref, acc_ref):
    tile = pl.program_id(0)
    rows = img_ref.shape[0]
    half = mine_ref.shape[0]
    wide = 256
    scale = scale_ref[0]
    shift = shift_ref[0]
    imgs = img_ref[...]
    loss_sum = jnp.zeros((8, 128), F32)
    scaled_sum = jnp.zeros((8, 128), F32)
    grad_sum = jnp.zeros((8, 128), F32)
    for side, txt_ref in enumerate((mine_ref, theirs_ref)):
        for at in range(0, half, wide):
            cosine = lax.dot_general(
                imgs, txt_ref[at : at + wide, :], (((1,), (1,)), ((), ())), preferred_element_type=F32
            )
            scaled = scale * cosine
            logits = scaled + shift
            small = jnp.exp(-jnp.abs(logits))
            whole = 1.0 + small
            grad = jnp.where(logits >= 0.0, 1.0, small) / whole
            signed = logits
            if side == 0 and at == 0:
                row = lax.broadcasted_iota(jnp.int32, (rows, wide), 0) + (tile * rows - first_ref[0])
                col = lax.broadcasted_iota(jnp.int32, (rows, wide), 1)
                positive = (row == col) & (col < 64)
                signed = jnp.where(positive, -logits, logits)
                grad = jnp.where(positive, grad - 1.0, grad)
            loss_sum += lanes(fold_sum(jnp.maximum(signed, 0.0)) + jnp.log1p(fold_growth(small)))
            scaled_sum += lanes(fold_sum(grad * scaled))
            grad_sum += lanes(fold_sum(grad))
            grad_ref[:, side * half + at : side * half + at + wide] = grad.astype(BF16)

    @pl.when(tile == 0)
    def _():
        acc_ref[...] = jnp.zeros_like(acc_ref)

    acc_ref[0] += loss_sum
    acc_ref[1] += scaled_sum
    acc_ref[2] += grad_sum

    @pl.when(tile == pl.num_programs(0) - 1)
    def _():
        for k in range(3):
            sums_ref[k] = jnp.sum(acc_ref[k])


def pairs(first, scale, shift, imgs, mine, theirs):
    count, emb = imgs.shape
    half = mine.shape[0]
    rows = 256
    return pl.pallas_call(
        pair_kernel,
        grid=(count // rows,),
        in_specs=[
            SMEM,
            SMEM,
            SMEM,
            pl.BlockSpec((rows, emb), lambda i: (i, 0)),
            pl.BlockSpec((half, emb), lambda i: (0, 0)),
            pl.BlockSpec((half, emb), lambda i: (0, 0)),
        ],
        out_specs=[
            pl.BlockSpec((rows, 2 * half), lambda i: (i, 0)),
            SMEM,
        ],
        out_shape=[
            jax.ShapeDtypeStruct((count, 2 * half), BF16),
            jax.ShapeDtypeStruct((3,), F32),
        ],
        scratch_shapes=[pltpu.VMEM((3, 8, 128), F32)],
        compiler_params=PARAMS,
        cost_estimate=cost(2 * count * 2 * half * emb, 8 * 2**20),
    )(first, scale, shift, imgs, mine, theirs)


def project_kernel(scale_ref, rows_ref, total_ref, out_ref):
    unit, norms = unit_of(rows_ref)
    direction = scale_ref[0] * total_ref[...]
    along = jnp.sum(direction * unit, axis=-1, keepdims=True)
    out_ref[...] = (direction - unit * along) / norms


def projected(scale, rows, total):
    return pl.pallas_call(
        project_kernel,
        in_specs=[SMEM, VMEM, VMEM],
        out_specs=VMEM,
        out_shape=jax.ShapeDtypeStruct(rows.shape, F32),
        compiler_params=PARAMS,
        cost_estimate=cost(10**6, 4 * 2**20),
    )(scale, rows, total)


def on_device(images, texts, log_scale, bias):
    rows, emb = images.shape
    scale = jnp.exp(log_scale)
    plane = (lax.axis_index("x_hi") * 4 + lax.axis_index("y")) * 2 + lax.axis_index("x_lo")
    first = (plane * rows).astype(jnp.int32).reshape(1)

    copies = pl.pallas_call(
        copies_kernel,
        in_specs=[VMEM],
        out_specs=VMEM,
        out_shape=jax.ShapeDtypeStruct((PEERS, rows, emb), BF16),
        compiler_params=PARAMS,
        cost_estimate=cost(10**6, 3 * 2**20),
    )(images)
    copies, texts_later = lax.optimization_barrier((copies, texts))
    txt_low = pl.pallas_call(
        low_kernel,
        in_specs=[VMEM],
        out_specs=VMEM,
        out_shape=jax.ShapeDtypeStruct((rows, emb), BF16),
        compiler_params=PARAMS,
        cost_estimate=cost(10**6, 2**19),
    )(texts_later)

    imgs = lax.all_to_all(copies, PLANE, 0, 0).reshape(PEERS * rows, emb)
    up, down = [txt_low], []
    for _ in range(4):
        up.append(along_z(up[-1], 1))
    down.append(along_z(txt_low, -1))
    for _ in range(2):
        down.append(along_z(down[-1], -1))
    mine = jnp.concatenate(up + down[::-1], axis=0)
    theirs = other_core(mine)

    grad_low, sums = pairs(first, scale, bias, imgs, mine, theirs)
    half = DEPTH * rows

    arrived = [moved(sums, by, 0) for by in (1, 2, 3)]
    txt_part = lax.dot_general(grad_low, imgs, (((0,), (0,)), ((), ())), preferred_element_type=F32)
    txt_part, grad_low, *arrived = lax.optimization_barrier((txt_part, grad_low, *arrived))
    theirs_part = other_core(coded(txt_part[half:])).reshape(DEPTH, rows, emb)
    mine_part = txt_part[:half].reshape(DEPTH, rows, emb)
    sums = sums + arrived[0] + arrived[1] + arrived[2]

    arrived = [moved(sums, 0, by) for by in (1, 2, 3)]
    img_part = jnp.dot(grad_low[:, :half], mine, preferred_element_type=F32) + jnp.dot(
        grad_low[:, half:], theirs, preferred_element_type=F32
    )
    img_part = coded(img_part).reshape(PEERS, rows, emb)
    img_part, *arrived = lax.optimization_barrier((img_part, *arrived))
    img_recv = lax.all_to_all(img_part, PLANE, 0, 0)
    sums = sums + arrived[0] + arrived[1] + arrived[2]
    sums = (sums + flipped(sums, 2, 1)) / (PAIRS * PEERS)

    riding = jnp.broadcast_to(jnp.pad(sums, (0, EXTRA - 3))[:, None], (EXTRA, emb))

    def block(k):
        return jnp.concatenate([mine_part[k] + decoded(theirs_part[k]), riding], axis=0)

    far = [along_z(coded(block(4)), -2), along_z(coded(block(5)), 2), along_z(coded(block(3)), -2)]
    near = [
        along_z(coded(block(6)), 2),
        along_z(coded(block(2) + decoded(far[0])), -2),
        along_z(coded(block(7) + decoded(far[1])), 1),
        along_z(coded(block(1) + decoded(far[2])), -1),
    ]
    total = block(0) + decoded(near[0]) + decoded(near[1]) + decoded(near[2]) + decoded(near[3])
    txt_total = total[:rows]
    stats = total[rows : rows + 3, 0] * (PAIRS * PEERS / (rows * 256))
    img_total = jnp.sum(decoded(img_recv), axis=0)

    image_grad = projected(scale, images, img_total)
    text_grad = projected(scale, texts, txt_total)
    return image_grad, text_grad, stats


def solution(mesh):
    fine = Mesh(mesh.devices.reshape(SIZES), AXES)
    whole = P(AXES, None)
    return jax.shard_map(
        on_device, mesh=fine, in_specs=(whole, whole, P(), P()), out_specs=(whole, whole, P()), check_vma=False
    )
```

```python
import jax
import jax.numpy as jnp
from jax import lax
from jax.experimental import pallas as pl
from jax.experimental.pallas import tpu as pltpu
from jax.sharding import Mesh
from jax.sharding import PartitionSpec as P

EPS = 1e-06
AXES = ("x_hi", "z", "core", "y", "x_lo")
SIZES = (2, 8, 2, 4, 2)
PLANE = ("x_hi", "y", "x_lo")
PEERS = 16
DEPTH = 8
CODE = 512.0
EXTRA = 8
PAIRS = 1024.0 * 1024.0
BF16 = jnp.bfloat16
F32 = jnp.float32
F16 = jnp.float16
VMEM = pl.BlockSpec(memory_space=pltpu.VMEM)
SMEM = pl.BlockSpec(memory_space=pltpu.SMEM)
PARAMS = pltpu.CompilerParams(vmem_limit_bytes=48 * 1024 * 1024)


def cost(flops, nbytes):
    return pl.CostEstimate(flops=flops, bytes_accessed=nbytes, transcendentals=0)


def place(index):
    out = []
    for size in reversed(SIZES):
        out.append(index % size)
        index //= size
    return list(reversed(out))


def number(where):
    index = 0
    for size, at in zip(SIZES, where):
        index = index * size + at
    return index


def shifted(array, axis, by):
    pairs = []
    for source in range(256):
        where = place(source)
        where[axis] = (where[axis] + by) % SIZES[axis]
        pairs.append((source, number(where)))
    return lax.ppermute(array, AXES, pairs)


def flipped(array, axis, by):
    pairs = []
    for source in range(256):
        where = place(source)
        where[axis] ^= by
        pairs.append((source, number(where)))
    return lax.ppermute(array, AXES, pairs)


def moved(array, dx, dy):
    pairs = []
    for source in range(256):
        x_hi, z, core, y, x_lo = place(source)
        x = (x_hi * 2 + x_lo + dx) % 4
        pairs.append((source, number((x // 2, z, core, (y + dy) % 4, x % 2))))
    return lax.ppermute(array, AXES, pairs)


def coded(array):
    return (array * lax.rsqrt(jnp.maximum(jnp.abs(array), 1e-36)) * CODE).astype(F16)


def decoded(array):
    wide = array.astype(F32) * (1.0 / CODE)
    return wide * jnp.abs(wide)


def along_z(array, by):
    return shifted(array, 1, by)


def other_core(array):
    return shifted(array, 2, 1)


def unit_of(ref):
    values = ref[...].astype(F32)
    norms = jnp.sqrt(jnp.sum(values * values, axis=-1, keepdims=True) + EPS)
    return values / norms, norms


def copies_kernel(rows_ref, out_ref):
    low = unit_of(rows_ref)[0].astype(BF16)
    for k in range(PEERS):
        out_ref[k] = low


def low_kernel(rows_ref, out_ref):
    out_ref[...] = unit_of(rows_ref)[0].astype(BF16)


def fold_sum(array):
    return jnp.sum(array.reshape(-1, 8, array.shape[-1]), axis=0)


def fold_growth(array):
    parts = array.reshape(-1, 8, array.shape[-1])
    while parts.shape[0] > 1:
        half = parts.shape[0] // 2
        a, b = parts[:half], parts[half:]
        parts = a + (b + a * b)
    return parts[0]


def lanes(array):
    out = array[:, :128]
    for at in range(128, array.shape[-1], 128):
        out = out + array[:, at : at + 128]
    return out


def pair_kernel(first_ref, scale_ref, shift_ref, img_ref, mine_ref, theirs_ref, grad_ref, sums_ref, acc_ref):
    tile = pl.program_id(0)
    rows = img_ref.shape[0]
    half = mine_ref.shape[0]
    wide = 256
    scale = scale_ref[0]
    shift = shift_ref[0]
    imgs = img_ref[...]
    loss_sum = jnp.zeros((8, 128), F32)
    scaled_sum = jnp.zeros((8, 128), F32)
    grad_sum = jnp.zeros((8, 128), F32)
    for side, txt_ref in enumerate((mine_ref, theirs_ref)):
        for at in range(0, half, wide):
            cosine = lax.dot_general(
                imgs, txt_ref[at : at + wide, :], (((1,), (1,)), ((), ())), preferred_element_type=F32
            )
            scaled = scale * cosine
            logits = scaled + shift
            small = jnp.exp(-jnp.abs(logits))
            whole = 1.0 + small
            grad = jnp.where(logits >= 0.0, 1.0, small) / whole
            signed = logits
            if side == 0 and at == 0:
                row = lax.broadcasted_iota(jnp.int32, (rows, wide), 0) + (tile * rows - first_ref[0])
                col = lax.broadcasted_iota(jnp.int32, (rows, wide), 1)
                positive = (row == col) & (col < 64)
                signed = jnp.where(positive, -logits, logits)
                grad = jnp.where(positive, grad - 1.0, grad)
            loss_sum += lanes(fold_sum(jnp.maximum(signed, 0.0)) + jnp.log1p(fold_growth(small)))
            scaled_sum += lanes(fold_sum(grad * scaled))
            grad_sum += lanes(fold_sum(grad))
            grad_ref[:, side * half + at : side * half + at + wide] = grad.astype(BF16)

    @pl.when(tile == 0)
    def _():
        acc_ref[...] = jnp.zeros_like(acc_ref)

    acc_ref[0] += loss_sum
    acc_ref[1] += scaled_sum
    acc_ref[2] += grad_sum

    @pl.when(tile == pl.num_programs(0) - 1)
    def _():
        for k in range(3):
            sums_ref[k] = jnp.sum(acc_ref[k])


def pairs(first, scale, shift, imgs, mine, theirs):
    count, emb = imgs.shape
    half = mine.shape[0]
    rows = 256
    return pl.pallas_call(
        pair_kernel,
        grid=(count // rows,),
        in_specs=[
            SMEM,
            SMEM,
            SMEM,
            pl.BlockSpec((rows, emb), lambda i: (i, 0)),
            pl.BlockSpec((half, emb), lambda i: (0, 0)),
            pl.BlockSpec((half, emb), lambda i: (0, 0)),
        ],
        out_specs=[
            pl.BlockSpec((rows, 2 * half), lambda i: (i, 0)),
            SMEM,
        ],
        out_shape=[
            jax.ShapeDtypeStruct((count, 2 * half), BF16),
            jax.ShapeDtypeStruct((3,), F32),
        ],
        scratch_shapes=[pltpu.VMEM((3, 8, 128), F32)],
        compiler_params=PARAMS,
        cost_estimate=cost(2 * count * 2 * half * emb, 8 * 2**20),
    )(first, scale, shift, imgs, mine, theirs)


def project_kernel(scale_ref, rows_ref, total_ref, out_ref):
    unit, norms = unit_of(rows_ref)
    direction = scale_ref[0] * total_ref[...]
    along = jnp.sum(direction * unit, axis=-1, keepdims=True)
    out_ref[...] = (direction - unit * along) / norms


def projected(scale, rows, total):
    return pl.pallas_call(
        project_kernel,
        in_specs=[SMEM, VMEM, VMEM],
        out_specs=VMEM,
        out_shape=jax.ShapeDtypeStruct(rows.shape, F32),
        compiler_params=PARAMS,
        cost_estimate=cost(10**6, 4 * 2**20),
    )(scale, rows, total)


def on_device(images, texts, log_scale, bias):
    rows, emb = images.shape
    scale = jnp.exp(log_scale)
    plane = (lax.axis_index("x_hi") * 4 + lax.axis_index("y")) * 2 + lax.axis_index("x_lo")
    first = (plane * rows).astype(jnp.int32).reshape(1)

    copies = pl.pallas_call(
        copies_kernel,
        in_specs=[VMEM],
        out_specs=VMEM,
        out_shape=jax.ShapeDtypeStruct((PEERS, rows, emb), BF16),
        compiler_params=PARAMS,
        cost_estimate=cost(10**6, 3 * 2**20),
    )(images)
    txt_low = pl.pallas_call(
        low_kernel,
        in_specs=[VMEM],
        out_specs=VMEM,
        out_shape=jax.ShapeDtypeStruct((rows, emb), BF16),
        compiler_params=PARAMS,
        cost_estimate=cost(10**6, 2**19),
    )(texts)

    imgs = lax.all_to_all(copies, PLANE, 0, 0).reshape(PEERS * rows, emb)
    up, down = [txt_low], []
    for _ in range(4):
        up.append(along_z(up[-1], 1))
    down.append(along_z(txt_low, -1))
    for _ in range(2):
        down.append(along_z(down[-1], -1))
    mine = jnp.concatenate(up + down[::-1], axis=0)
    theirs = other_core(mine)

    grad_low, sums = pairs(first, scale, bias, imgs, mine, theirs)
    half = DEPTH * rows

    arrived = [moved(sums, by, 0) for by in (1, 2, 3)]
    txt_part = lax.dot_general(grad_low, imgs, (((0,), (0,)), ((), ())), preferred_element_type=F32)
    txt_part, grad_low, *arrived = lax.optimization_barrier((txt_part, grad_low, *arrived))
    theirs_part = other_core(coded(txt_part[half:])).reshape(DEPTH, rows, emb)
    mine_part = txt_part[:half].reshape(DEPTH, rows, emb)
    sums = sums + arrived[0] + arrived[1] + arrived[2]

    arrived = [moved(sums, 0, by) for by in (1, 2, 3)]
    img_part = jnp.dot(grad_low[:, :half], mine, preferred_element_type=F32) + jnp.dot(
        grad_low[:, half:], theirs, preferred_element_type=F32
    )
    img_part = coded(img_part).reshape(PEERS, rows, emb)
    img_part, *arrived = lax.optimization_barrier((img_part, *arrived))
    img_recv = lax.all_to_all(img_part, PLANE, 0, 0)
    sums = sums + arrived[0] + arrived[1] + arrived[2]
    sums = (sums + flipped(sums, 2, 1)) / (PAIRS * PEERS)

    riding = jnp.broadcast_to(jnp.pad(sums, (0, EXTRA - 3))[:, None], (EXTRA, emb))

    def block(k):
        return jnp.concatenate([mine_part[k] + decoded(theirs_part[k]), riding], axis=0)

    far = [along_z(coded(block(4)), -2), along_z(coded(block(5)), 2), along_z(coded(block(3)), -2)]
    near = [
        along_z(coded(block(6)), 2),
        along_z(coded(block(2) + decoded(far[0])), -2),
        along_z(coded(block(7) + decoded(far[1])), 1),
        along_z(coded(block(1) + decoded(far[2])), -1),
    ]
    total = block(0) + decoded(near[0]) + decoded(near[1]) + decoded(near[2]) + decoded(near[3])
    txt_total = total[:rows]
    stats = total[rows : rows + 3, 0] * (PAIRS * PEERS / (rows * 256))
    img_total = jnp.sum(decoded(img_recv), axis=0)

    image_grad = projected(scale, images, img_total)
    text_grad = projected(scale, texts, txt_total)
    return image_grad, text_grad, stats


def solution(mesh):
    fine = Mesh(mesh.devices.reshape(SIZES), AXES)
    whole = P(AXES, None)
    return jax.shard_map(
        on_device, mesh=fine, in_specs=(whole, whole, P(), P()), out_specs=(whole, whole, P()), check_vma=False
    )
```

```python
import jax
import jax.numpy as jnp
from jax import lax
from jax.experimental import pallas as pl
from jax.experimental.pallas import tpu as pltpu
from jax.sharding import Mesh
from jax.sharding import PartitionSpec as P

EPS = 1e-06
AXES = ("x_hi", "z", "core", "y", "x_lo")
SIZES = (2, 8, 2, 4, 2)
PLANE = ("x_hi", "y", "x_lo")
PEERS = 16
DEPTH = 8
CODE = 512.0
EXTRA = 8
PAIRS = 1024.0 * 1024.0
BF16 = jnp.bfloat16
F32 = jnp.float32
F16 = jnp.float16
VMEM = pl.BlockSpec(memory_space=pltpu.VMEM)
SMEM = pl.BlockSpec(memory_space=pltpu.SMEM)
PARAMS = pltpu.CompilerParams(vmem_limit_bytes=48 * 1024 * 1024)


def cost(flops, nbytes):
    return pl.CostEstimate(flops=flops, bytes_accessed=nbytes, transcendentals=0)


def place(index):
    out = []
    for size in reversed(SIZES):
        out.append(index % size)
        index //= size
    return list(reversed(out))


def number(where):
    index = 0
    for size, at in zip(SIZES, where):
        index = index * size + at
    return index


def shifted(array, axis, by):
    pairs = []
    for source in range(256):
        where = place(source)
        where[axis] = (where[axis] + by) % SIZES[axis]
        pairs.append((source, number(where)))
    return lax.ppermute(array, AXES, pairs)


def flipped(array, axis, by):
    pairs = []
    for source in range(256):
        where = place(source)
        where[axis] ^= by
        pairs.append((source, number(where)))
    return lax.ppermute(array, AXES, pairs)


def moved(array, dx, dy):
    pairs = []
    for source in range(256):
        x_hi, z, core, y, x_lo = place(source)
        x = (x_hi * 2 + x_lo + dx) % 4
        pairs.append((source, number((x // 2, z, core, (y + dy) % 4, x % 2))))
    return lax.ppermute(array, AXES, pairs)


def coded(array):
    return (array * lax.rsqrt(jnp.maximum(jnp.abs(array), 1e-36)) * CODE).astype(F16)


def decoded(array):
    wide = array.astype(F32) * (1.0 / CODE)
    return wide * jnp.abs(wide)


def along_z(array, by):
    return shifted(array, 1, by)


def other_core(array):
    return shifted(array, 2, 1)


def unit_of(ref):
    values = ref[...].astype(F32)
    norms = jnp.sqrt(jnp.sum(values * values, axis=-1, keepdims=True) + EPS)
    return values / norms, norms


def copies_kernel(rows_ref, out_ref):
    low = unit_of(rows_ref)[0].astype(BF16)
    for k in range(PEERS):
        out_ref[k] = low


def low_kernel(rows_ref, out_ref):
    out_ref[...] = unit_of(rows_ref)[0].astype(BF16)


def fold_sum(array):
    return jnp.sum(array.reshape(-1, 8, array.shape[-1]), axis=0)


def fold_growth(array):
    parts = array.reshape(-1, 8, array.shape[-1])
    while parts.shape[0] > 1:
        half = parts.shape[0] // 2
        a, b = parts[:half], parts[half:]
        parts = a + (b + a * b)
    return parts[0]


def lanes(array):
    out = array[:, :128]
    for at in range(128, array.shape[-1], 128):
        out = out + array[:, at : at + 128]
    return out


def pair_kernel(first_ref, scale_ref, shift_ref, img_ref, mine_ref, theirs_ref, grad_ref, sums_ref, acc_ref):
    tile = pl.program_id(0)
    rows = img_ref.shape[0]
    half = mine_ref.shape[0]
    wide = 256
    scale = scale_ref[0]
    shift = shift_ref[0]
    imgs = img_ref[...]
    loss_sum = jnp.zeros((8, 128), F32)
    scaled_sum = jnp.zeros((8, 128), F32)
    grad_sum = jnp.zeros((8, 128), F32)
    for side, txt_ref in enumerate((mine_ref, theirs_ref)):
        for at in range(0, half, wide):
            cosine = lax.dot_general(
                imgs, txt_ref[at : at + wide, :], (((1,), (1,)), ((), ())), preferred_element_type=F32
            )
            scaled = scale * cosine
            logits = scaled + shift
            small = jnp.exp(-jnp.abs(logits))
            whole = 1.0 + small
            grad = jnp.where(logits >= 0.0, 1.0, small) / whole
            signed = logits
            if side == 0 and at == 0:
                row = lax.broadcasted_iota(jnp.int32, (rows, wide), 0) + (tile * rows - first_ref[0])
                col = lax.broadcasted_iota(jnp.int32, (rows, wide), 1)
                positive = (row == col) & (col < 64)
                signed = jnp.where(positive, -logits, logits)
                grad = jnp.where(positive, grad - 1.0, grad)
            loss_sum += lanes(fold_sum(jnp.maximum(signed, 0.0)) + jnp.log1p(fold_growth(small)))
            scaled_sum += lanes(fold_sum(grad * scaled))
            grad_sum += lanes(fold_sum(grad))
            grad_ref[:, side * half + at : side * half + at + wide] = grad.astype(BF16)

    @pl.when(tile == 0)
    def _():
        acc_ref[...] = jnp.zeros_like(acc_ref)

    acc_ref[0] += loss_sum
    acc_ref[1] += scaled_sum
    acc_ref[2] += grad_sum

    @pl.when(tile == pl.num_programs(0) - 1)
    def _():
        for k in range(3):
            sums_ref[k] = jnp.sum(acc_ref[k])


def pairs(first, scale, shift, imgs, txts):
    count, emb = imgs.shape
    half = txts.shape[0] // 2
    rows = 256
    return pl.pallas_call(
        pair_kernel,
        grid=(count // rows,),
        in_specs=[
            SMEM,
            SMEM,
            SMEM,
            pl.BlockSpec((rows, emb), lambda i: (i, 0)),
            pl.BlockSpec((half, emb), lambda i: (0, 0)),
            pl.BlockSpec((half, emb), lambda i: (1, 0)),
        ],
        out_specs=[
            pl.BlockSpec((rows, 2 * half), lambda i: (i, 0)),
            SMEM,
        ],
        out_shape=[
            jax.ShapeDtypeStruct((count, 2 * half), BF16),
            jax.ShapeDtypeStruct((3,), F32),
        ],
        scratch_shapes=[pltpu.VMEM((3, 8, 128), F32)],
        compiler_params=PARAMS,
        cost_estimate=cost(2 * count * 2 * half * emb, 8 * 2**20),
    )(first, scale, shift, imgs, txts, txts)


def project_kernel(scale_ref, rows_ref, total_ref, out_ref):
    unit, norms = unit_of(rows_ref)
    direction = scale_ref[0] * total_ref[...]
    along = jnp.sum(direction * unit, axis=-1, keepdims=True)
    out_ref[...] = (direction - unit * along) / norms


def projected(scale, rows, total):
    return pl.pallas_call(
        project_kernel,
        in_specs=[SMEM, VMEM, VMEM],
        out_specs=VMEM,
        out_shape=jax.ShapeDtypeStruct(rows.shape, F32),
        compiler_params=PARAMS,
        cost_estimate=cost(10**6, 4 * 2**20),
    )(scale, rows, total)


def on_device(images, texts, log_scale, bias):
    rows, emb = images.shape
    scale = jnp.exp(log_scale)
    plane = (lax.axis_index("x_hi") * 4 + lax.axis_index("y")) * 2 + lax.axis_index("x_lo")
    first = (plane * rows).astype(jnp.int32).reshape(1)

    copies = pl.pallas_call(
        copies_kernel,
        in_specs=[VMEM],
        out_specs=VMEM,
        out_shape=jax.ShapeDtypeStruct((PEERS, rows, emb), BF16),
        compiler_params=PARAMS,
        cost_estimate=cost(10**6, 3 * 2**20),
    )(images)
    txt_low = pl.pallas_call(
        low_kernel,
        in_specs=[VMEM],
        out_specs=VMEM,
        out_shape=jax.ShapeDtypeStruct((rows, emb), BF16),
        compiler_params=PARAMS,
        cost_estimate=cost(10**6, 2**19),
    )(texts)

    imgs = lax.all_to_all(copies, PLANE, 0, 0).reshape(PEERS * rows, emb)
    up, down = [txt_low], []
    for _ in range(4):
        up.append(along_z(up[-1], 1))
    down.append(along_z(txt_low, -1))
    for _ in range(2):
        down.append(along_z(down[-1], -1))
    mine = jnp.concatenate(up + down[::-1], axis=0)
    theirs = other_core(mine)

    txts = jnp.concatenate([mine, theirs], axis=0)
    grad_low, sums = pairs(first, scale, bias, imgs, txts)
    half = DEPTH * rows

    arrived = [moved(sums, by, 0) for by in (1, 2, 3)]
    txt_part = lax.dot_general(grad_low, imgs, (((0,), (0,)), ((), ())), preferred_element_type=F32)
    txt_part, grad_low, *arrived = lax.optimization_barrier((txt_part, grad_low, *arrived))
    theirs_part = other_core(coded(txt_part[half:])).reshape(DEPTH, rows, emb)
    mine_part = txt_part[:half].reshape(DEPTH, rows, emb)
    sums = sums + arrived[0] + arrived[1] + arrived[2]

    arrived = [moved(sums, 0, by) for by in (1, 2, 3)]
    img_part = jnp.dot(grad_low, txts, preferred_element_type=F32)
    img_part = coded(img_part).reshape(PEERS, rows, emb)
    img_part, *arrived = lax.optimization_barrier((img_part, *arrived))
    img_recv = lax.all_to_all(img_part, PLANE, 0, 0)
    sums = sums + arrived[0] + arrived[1] + arrived[2]
    sums = (sums + flipped(sums, 2, 1)) / (PAIRS * PEERS)

    riding = jnp.broadcast_to(jnp.pad(sums, (0, EXTRA - 3))[:, None], (EXTRA, emb))

    def block(k):
        return jnp.concatenate([mine_part[k] + decoded(theirs_part[k]), riding], axis=0)

    far = [along_z(coded(block(4)), -2), along_z(coded(block(5)), 2), along_z(coded(block(3)), -2)]
    near = [
        along_z(coded(block(6)), 2),
        along_z(coded(block(2) + decoded(far[0])), -2),
        along_z(coded(block(7) + decoded(far[1])), 1),
        along_z(coded(block(1) + decoded(far[2])), -1),
    ]
    total = block(0) + decoded(near[0]) + decoded(near[1]) + decoded(near[2]) + decoded(near[3])
    txt_total = total[:rows]
    stats = total[rows : rows + 3, 0] * (PAIRS * PEERS / (rows * 256))
    img_total = jnp.sum(decoded(img_recv), axis=0)

    image_grad = projected(scale, images, img_total)
    text_grad = projected(scale, texts, txt_total)
    return image_grad, text_grad, stats


def solution(mesh):
    fine = Mesh(mesh.devices.reshape(SIZES), AXES)
    whole = P(AXES, None)
    return jax.shard_map(
        on_device, mesh=fine, in_specs=(whole, whole, P(), P()), out_specs=(whole, whole, P()), check_vma=False
    )
```

```python
import jax
import jax.numpy as jnp
from jax import lax
from jax.experimental import pallas as pl
from jax.experimental.pallas import tpu as pltpu
from jax.sharding import Mesh
from jax.sharding import PartitionSpec as P

EPS = 1e-06
AXES = ("x_hi", "z", "core", "y", "x_lo")
SIZES = (2, 8, 2, 4, 2)
PLANE = ("x_hi", "y", "x_lo")
PEERS = 16
DEPTH = 8
CODE = 512.0
EXTRA = 8
PAIRS = 1024.0 * 1024.0
BF16 = jnp.bfloat16
F32 = jnp.float32
F16 = jnp.float16
VMEM = pl.BlockSpec(memory_space=pltpu.VMEM)
SMEM = pl.BlockSpec(memory_space=pltpu.SMEM)
PARAMS = pltpu.CompilerParams(vmem_limit_bytes=48 * 1024 * 1024)


def cost(flops, nbytes):
    return pl.CostEstimate(flops=flops, bytes_accessed=nbytes, transcendentals=0)


def place(index):
    out = []
    for size in reversed(SIZES):
        out.append(index % size)
        index //= size
    return list(reversed(out))


def number(where):
    index = 0
    for size, at in zip(SIZES, where):
        index = index * size + at
    return index


def shifted(array, axis, by):
    pairs = []
    for source in range(256):
        where = place(source)
        where[axis] = (where[axis] + by) % SIZES[axis]
        pairs.append((source, number(where)))
    return lax.ppermute(array, AXES, pairs)


def flipped(array, axis, by):
    pairs = []
    for source in range(256):
        where = place(source)
        where[axis] ^= by
        pairs.append((source, number(where)))
    return lax.ppermute(array, AXES, pairs)


def moved(array, dx, dy):
    pairs = []
    for source in range(256):
        x_hi, z, core, y, x_lo = place(source)
        x = (x_hi * 2 + x_lo + dx) % 4
        pairs.append((source, number((x // 2, z, core, (y + dy) % 4, x % 2))))
    return lax.ppermute(array, AXES, pairs)


def coded(array):
    return (array * lax.rsqrt(jnp.maximum(jnp.abs(array), 1e-36)) * CODE).astype(F16)


def decoded(array):
    wide = array.astype(F32) * (1.0 / CODE)
    return wide * jnp.abs(wide)


def along_z(array, by):
    return shifted(array, 1, by)


def other_core(array):
    return shifted(array, 2, 1)


def unit_of(ref):
    values = ref[...].astype(F32)
    norms = jnp.sqrt(jnp.sum(values * values, axis=-1, keepdims=True) + EPS)
    return values / norms, norms


def copies_kernel(rows_ref, out_ref):
    low = unit_of(rows_ref)[0].astype(BF16)
    for k in range(PEERS):
        out_ref[k] = low


def low_kernel(rows_ref, out_ref):
    out_ref[...] = unit_of(rows_ref)[0].astype(BF16)


def fold_sum(array):
    return jnp.sum(array.reshape(-1, 8, array.shape[-1]), axis=0)


def fold_growth(array):
    parts = array.reshape(-1, 8, array.shape[-1])
    while parts.shape[0] > 1:
        half = parts.shape[0] // 2
        a, b = parts[:half], parts[half:]
        parts = a + (b + a * b)
    return parts[0]


def lanes(array):
    out = array[:, :128]
    for at in range(128, array.shape[-1], 128):
        out = out + array[:, at : at + 128]
    return out


def pair_kernel(first_ref, scale_ref, shift_ref, img_ref, mine_ref, theirs_ref, grad_ref, sums_ref, acc_ref):
    tile = pl.program_id(0)
    rows = img_ref.shape[0]
    half = mine_ref.shape[0]
    wide = 256
    scale = scale_ref[0]
    shift = shift_ref[0]
    imgs = img_ref[...]
    loss_sum = jnp.zeros((8, 128), F32)
    scaled_sum = jnp.zeros((8, 128), F32)
    grad_sum = jnp.zeros((8, 128), F32)
    for side, txt_ref in enumerate((mine_ref, theirs_ref)):
        for at in range(0, half, wide):
            cosine = lax.dot_general(
                imgs, txt_ref[at : at + wide, :], (((1,), (1,)), ((), ())), preferred_element_type=F32
            )
            scaled = scale * cosine
            logits = scaled + shift
            small = jnp.exp(-jnp.abs(logits))
            whole = 1.0 + small
            grad = jnp.where(logits >= 0.0, 1.0, small) / whole
            signed = logits
            if side == 0 and at == 0:
                row = lax.broadcasted_iota(jnp.int32, (rows, wide), 0) + (tile * rows - first_ref[0])
                col = lax.broadcasted_iota(jnp.int32, (rows, wide), 1)
                positive = (row == col) & (col < 64)
                signed = jnp.where(positive, -logits, logits)
                grad = jnp.where(positive, grad - 1.0, grad)
            loss_sum += lanes(fold_sum(jnp.maximum(signed, 0.0)) + jnp.log1p(fold_growth(small)))
            scaled_sum += lanes(fold_sum(grad * scaled))
            grad_sum += lanes(fold_sum(grad))
            grad_ref[:, side * half + at : side * half + at + wide] = grad.astype(BF16)

    @pl.when(tile == 0)
    def _():
        acc_ref[...] = jnp.zeros_like(acc_ref)

    acc_ref[0] += loss_sum
    acc_ref[1] += scaled_sum
    acc_ref[2] += grad_sum

    @pl.when(tile == pl.num_programs(0) - 1)
    def _():
        for k in range(3):
            sums_ref[k] = jnp.sum(acc_ref[k])


def pairs(first, scale, shift, imgs, txts):
    count, emb = imgs.shape
    half = txts.shape[0] // 2
    rows = 512
    return pl.pallas_call(
        pair_kernel,
        grid=(count // rows,),
        in_specs=[
            SMEM,
            SMEM,
            SMEM,
            pl.BlockSpec((rows, emb), lambda i: (i, 0)),
            pl.BlockSpec((half, emb), lambda i: (0, 0)),
            pl.BlockSpec((half, emb), lambda i: (1, 0)),
        ],
        out_specs=[
            pl.BlockSpec((rows, 2 * half), lambda i: (i, 0)),
            SMEM,
        ],
        out_shape=[
            jax.ShapeDtypeStruct((count, 2 * half), BF16),
            jax.ShapeDtypeStruct((3,), F32),
        ],
        scratch_shapes=[pltpu.VMEM((3, 8, 128), F32)],
        compiler_params=PARAMS,
        cost_estimate=cost(2 * count * 2 * half * emb, 8 * 2**20),
    )(first, scale, shift, imgs, txts, txts)


def project_kernel(scale_ref, rows_ref, total_ref, out_ref):
    unit, norms = unit_of(rows_ref)
    direction = scale_ref[0] * total_ref[...]
    along = jnp.sum(direction * unit, axis=-1, keepdims=True)
    out_ref[...] = (direction - unit * along) / norms


def projected(scale, rows, total):
    return pl.pallas_call(
        project_kernel,
        in_specs=[SMEM, VMEM, VMEM],
        out_specs=VMEM,
        out_shape=jax.ShapeDtypeStruct(rows.shape, F32),
        compiler_params=PARAMS,
        cost_estimate=cost(10**6, 4 * 2**20),
    )(scale, rows, total)


def on_device(images, texts, log_scale, bias):
    rows, emb = images.shape
    scale = jnp.exp(log_scale)
    plane = (lax.axis_index("x_hi") * 4 + lax.axis_index("y")) * 2 + lax.axis_index("x_lo")
    first = (plane * rows).astype(jnp.int32).reshape(1)

    copies = pl.pallas_call(
        copies_kernel,
        in_specs=[VMEM],
        out_specs=VMEM,
        out_shape=jax.ShapeDtypeStruct((PEERS, rows, emb), BF16),
        compiler_params=PARAMS,
        cost_estimate=cost(10**6, 3 * 2**20),
    )(images)
    txt_low = pl.pallas_call(
        low_kernel,
        in_specs=[VMEM],
        out_specs=VMEM,
        out_shape=jax.ShapeDtypeStruct((rows, emb), BF16),
        compiler_params=PARAMS,
        cost_estimate=cost(10**6, 2**19),
    )(texts)

    imgs = lax.all_to_all(copies, PLANE, 0, 0).reshape(PEERS * rows, emb)
    up, down = [txt_low], []
    for _ in range(4):
        up.append(along_z(up[-1], 1))
    down.append(along_z(txt_low, -1))
    for _ in range(2):
        down.append(along_z(down[-1], -1))
    mine = jnp.concatenate(up + down[::-1], axis=0)
    theirs = other_core(mine)

    txts = jnp.concatenate([mine, theirs], axis=0)
    grad_low, sums = pairs(first, scale, bias, imgs, txts)
    half = DEPTH * rows

    arrived = [moved(sums, by, 0) for by in (1, 2, 3)]
    txt_part = lax.dot_general(grad_low, imgs, (((0,), (0,)), ((), ())), preferred_element_type=F32)
    txt_part, grad_low, *arrived = lax.optimization_barrier((txt_part, grad_low, *arrived))
    theirs_part = other_core(coded(txt_part[half:])).reshape(DEPTH, rows, emb)
    mine_part = txt_part[:half].reshape(DEPTH, rows, emb)
    sums = sums + arrived[0] + arrived[1] + arrived[2]

    arrived = [moved(sums, 0, by) for by in (1, 2, 3)]
    img_part = jnp.dot(grad_low, txts, preferred_element_type=F32)
    img_part = coded(img_part).reshape(PEERS, rows, emb)
    img_part, *arrived = lax.optimization_barrier((img_part, *arrived))
    img_recv = lax.all_to_all(img_part, PLANE, 0, 0)
    sums = sums + arrived[0] + arrived[1] + arrived[2]
    sums = (sums + flipped(sums, 2, 1)) / (PAIRS * PEERS)

    riding = jnp.broadcast_to(jnp.pad(sums, (0, EXTRA - 3))[:, None], (EXTRA, emb))

    def block(k):
        return jnp.concatenate([mine_part[k] + decoded(theirs_part[k]), riding], axis=0)

    far = [along_z(coded(block(4)), -2), along_z(coded(block(5)), 2), along_z(coded(block(3)), -2)]
    near = [
        along_z(coded(block(6)), 2),
        along_z(coded(block(2) + decoded(far[0])), -2),
        along_z(coded(block(7) + decoded(far[1])), 1),
        along_z(coded(block(1) + decoded(far[2])), -1),
    ]
    total = block(0) + decoded(near[0]) + decoded(near[1]) + decoded(near[2]) + decoded(near[3])
    txt_total = total[:rows]
    stats = total[rows : rows + 3, 0] * (PAIRS * PEERS / (rows * 256))
    img_total = jnp.sum(decoded(img_recv), axis=0)

    image_grad = projected(scale, images, img_total)
    text_grad = projected(scale, texts, txt_total)
    return image_grad, text_grad, stats


def solution(mesh):
    fine = Mesh(mesh.devices.reshape(SIZES), AXES)
    whole = P(AXES, None)
    return jax.shard_map(
        on_device, mesh=fine, in_specs=(whole, whole, P(), P()), out_specs=(whole, whole, P()), check_vma=False
    )
```
